32 devices in a mesh: groups: 2 (over x), az: 16 (over z, y, core).
Axes of the slice: x: 2, y: 2, z: 4, core: 2. Of those that a mesh axis runs over, the one named last changes fastest.
Arguments:
- surface_nodes: bfloat16 [8, 16, 128, 2304], P('groups', 'az'), parts along dimension 0, may hold values from -6 to 6
- amplitudes: bfloat16 [16, 256, 4, 16, 128], P('groups', None, None, 'az'), parts along dimension 0, may hold values from -0.0625 to 0.0625
- block_offsets: int32 [16, 32], P('az', 'groups'), parts along dimension 1, may hold values from -1 to 248, as said below
- welch_first: int32 [512], P(('groups', 'az')), parts along dimension 0, may hold values from 0 to 512
Outputs:
- pressure: float32 [512, 2048], P(('groups', 'az')), parts along dimension 0
- spectra: float32 [512, 512], P(('groups', 'az')), parts along dimension 0
The draws below stay inside these ranges and needn't reach their ends.
There are 2 independent parts, one for each index of `groups`. The reference program is written for one: setup_inputs(seed, part) draws one part's arguments, and reference() takes and returns one part's arrays. A program takes and returns all parts, laid end to end along the dimension named above; each array names one. Nothing has to cross between parts.
Inputs may be any that keep to these rules, and one draw needn't show every extreme that they name: `block_offsets`: an entry of -1 marks a panel column and observer block whose contribution is left out; any other entry is the pair's coarse retarded-time offset in samples.
All inputs are finite; a program needn't handle non-finite values.
Results may differ from the reference program's by a relative error of at most 0.0003.
Values may be sent and summed in bfloat16 or wider, within the bound.
A program may use at most 64 MiB of HBM per device.

```python
import jax
import jax.numpy as jnp
from jax import lax

NAXIAL = 128
NO = 256
KTAPS = 8
HEAD = 256
SEG = 1024
NSEG = 2
NSAMP = 2048
NSRC = 2304
AZ = 16
NOB = 16
N_AZ = 16


def draw_block_offsets(key, part):
    column_ids = jnp.arange(AZ, dtype=jnp.int32)
    distance = jnp.minimum(column_ids, AZ - column_ids)
    nearness = AZ - 2 * distance
    threshold = AZ * AZ + 7 * nearness * nearness
    key_pick, key_offset = jax.random.split(key)
    picked = jax.random.randint(key_pick, (AZ, NOB), 0, 8 * AZ * AZ, dtype=jnp.int32)
    offsets = jax.random.randint(key_offset, (AZ, NOB), 0, HEAD - KTAPS + 1, dtype=jnp.int32)
    offsets = jnp.where(picked < threshold[:, None], offsets, -1)
    return offsets.at[0, 0].set(HEAD - KTAPS)


def touch_ends(result, rng, least, high):
    longest = result.shape.index(max(result.shape))
    spots = []
    for shift in (0, 1):
        where = [jax.random.randint(jax.random.fold_in(rng, axis), (), 0, length) for axis, length in enumerate(result.shape)]
        where[longest] = (where[longest] + shift) % result.shape[longest]
        spots.append(tuple(where))
    return result.at[spots[0]].set(least).at[spots[1]].set(high)


def with_spikes(entries, rng, source, target, blocks, factor):
    def block_of(dim):
        return (jnp.arange(entries.shape[dim]) // (entries.shape[dim] // blocks)).reshape((-1,) + (1,) * (entries.ndim - 1 - dim))

    near = jax.random.permutation(rng, blocks)[block_of(target)]
    second = (block_of(target) + blocks // 2) % blocks
    return jnp.where((block_of(source) == near) | (block_of(source) == second), factor * entries, entries)


def steps_of(stream_key, extent, shards, low, top_value):
    def one(position, shards_of):
        steps = jax.random.uniform(jax.random.fold_in(jax.random.fold_in(stream_key, 6), position), (shards_of,), jnp.float32, low / len(shards), top_value / len(shards))
        return jnp.repeat(jnp.exp(steps), extent[position] // shards_of).reshape((-1,) + (1,) * (len(extent) - position - 1))

    level = one(*shards[0])
    for cut in shards[1:]:
        level = level * one(*cut)
    return level


def normal_values(key, dims, width, limit, shards=(), held_as=jnp.bfloat16):
    result = jax.random.normal(key, dims, jnp.float32) * width
    if len(shards) > 0:
        result = steps_of(key, dims, shards, -0.22, 0.18) * result
    return jnp.clip(result, min=-limit, max=limit).astype(held_as)


def heavy_noise(stream_key, extent, scale, reach, shards, heavy, kind=jnp.bfloat16):
    values = scale * jax.random.normal(stream_key, extent, jnp.float32)
    if shards:
        values = values * steps_of(stream_key, extent, shards, -0.22, 0.18)
    return jnp.clip(with_spikes(values, jax.random.fold_in(stream_key, 3), *heavy), -reach, reach).astype(kind)


def setup_inputs(seed: int = 0, part: int = 0) -> dict:
    keys = jax.random.split(jax.random.key(seed), 5)
    part_splits = jax.random.split(jax.random.fold_in(keys[4], part), 5)
    return {
        "surface_nodes": normal_values(part_splits[0], (4, AZ, NAXIAL, NSRC), 1.0, 6.0, ((1, 16),)),
        "amplitudes": heavy_noise(part_splits[1], (KTAPS, NO, 4, AZ, NAXIAL), (KTAPS * NAXIAL * AZ) ** -0.5, 0.0625, ((3, 16),), (3, 1, 16, 2.0)),
        "block_offsets": draw_block_offsets(jax.random.fold_in(jax.random.fold_in(keys[4], part), 71), part),
        "welch_first": touch_ends(jax.random.randint(part_splits[3], (NO,), 0, SEG // 2 + 1), jax.random.fold_in(part_splits[3], 1), 0, (SEG // 2 + 1) - 1).astype(jnp.int32),
    }


def block_term(own_rows, next_rows, amp_rows, offset):
    observers = amp_rows.shape[0] // KTAPS

    def compute():
        delayed = jnp.dot(amp_rows, own_rows, preferred_element_type=jnp.float32) + jnp.dot(amp_rows, next_rows, preferred_element_type=jnp.float32)
        delayed = (0.5 * delayed).reshape(KTAPS, observers, NSRC)
        summed = jnp.zeros((observers, NSAMP), jnp.float32)
        for tap_index in range(KTAPS):
            begin = (HEAD - offset - tap_index).astype(jnp.int32)
            summed = summed + lax.dynamic_slice_in_dim(delayed[tap_index], begin, NSAMP, axis=1)
        return summed

    def skipped():
        return jnp.zeros((observers, NSAMP), jnp.float32)

    return lax.cond(offset >= 0, compute, skipped)


def welch_basis():
    sample_index = jnp.arange(SEG, dtype=jnp.int32)
    frequency = jnp.arange(SEG // 2, dtype=jnp.int32)
    phase_index = (sample_index[:, None] * frequency[None, :]) % SEG
    angles = (2.0 * jnp.pi / SEG) * phase_index.astype(jnp.float32)
    window = 0.5 - 0.5 * jnp.cos((2.0 * jnp.pi / SEG) * sample_index.astype(jnp.float32))
    dft_basis = jnp.concatenate([jnp.cos(angles), -jnp.sin(angles)], axis=1) * window[:, None]
    return dft_basis, jnp.sum(window * window)


def welch_spectra(pressure, welch_first):
    dft_basis, energy = welch_basis()
    half_seg = SEG // 2

    def slice_series(series, start_at):
        return jnp.stack([lax.dynamic_slice_in_dim(series, (start_at + segment_id * half_seg).astype(jnp.int32), SEG) for segment_id in range(NSEG)])

    segments = jax.vmap(slice_series)(pressure, welch_first)
    num_rows = pressure.shape[0]
    coeffs = jnp.dot(segments.reshape(num_rows * NSEG, SEG), dft_basis, precision=lax.Precision.HIGHEST, preferred_element_type=jnp.float32)
    power = coeffs[:, :half_seg] ** 2 + coeffs[:, half_seg:] ** 2
    return jnp.mean(power.reshape(num_rows, NSEG, half_seg), axis=1) / energy


def reference(surface_nodes, amplitudes, block_offsets, welch_first):
    columns = surface_nodes.shape[1]
    observers = NO // N_AZ
    node_stack = jnp.transpose(surface_nodes, (1, 0, 2, 3)).reshape(columns, 4 * NAXIAL, NSRC)
    next_stack = jnp.roll(node_stack, -1, axis=0)
    amp_stack = jnp.transpose(amplitudes, (3, 0, 1, 2, 4)).reshape(columns, KTAPS, NO, 4 * NAXIAL)

    def one_block(obs_block):
        def add_column(column, summed):
            chosen = lax.dynamic_slice_in_dim(amp_stack[column], (obs_block * observers).astype(jnp.int32), observers, axis=1)
            return summed + block_term(node_stack[column], next_stack[column], chosen.reshape(KTAPS * observers, 4 * NAXIAL), block_offsets[column, obs_block])

        return lax.fori_loop(0, columns, add_column, jnp.zeros((observers, NSAMP), jnp.float32))

    pressure = lax.map(one_block, jnp.arange(N_AZ, dtype=jnp.int32)).reshape(NO, NSAMP)
    spectra = welch_spectra(pressure, welch_first)
    return pressure, spectra
```

```python
import functools

import jax
import jax.numpy as jnp
import ml_dtypes
import numpy as np
from jax import lax
from jax.experimental import pallas as pl
from jax.experimental.pallas import tpu as pltpu
from jax.sharding import PartitionSpec as P

NAXIAL = 128
NO = 256
KTAPS = 8
HEAD = 256
SEG = 1024
NSEG = 2
NSAMP = 2048


def shifted(block, axis, distance):
    devices = range(lax.axis_size(axis))
    route = [((i - distance) % len(devices), i) for i in devices]
    return lax.ppermute(block, axis, route)


def pair_term(node_list, amp_rows, offset, length):
    observers = amp_rows.shape[0] // KTAPS

    def compute():
        delayed = jnp.zeros((amp_rows.shape[0], length + HEAD), jnp.float32)
        for node_rows in node_list:
            delayed = delayed + jnp.dot(amp_rows, node_rows, preferred_element_type=jnp.float32)
        delayed = (0.5 * delayed).reshape(KTAPS, observers, length + HEAD)
        summed = jnp.zeros((observers, length), jnp.float32)
        for tap_index in range(KTAPS):
            summed = summed + lax.dynamic_slice_in_dim(
                delayed[tap_index], HEAD - offset - tap_index, length, axis=1
            )
        return summed

    def skipped():
        return jnp.zeros((observers, length), jnp.float32)

    return lax.cond(offset >= 0, compute, skipped)


def welch_basis():
    sample_index = jnp.arange(SEG, dtype=jnp.int32)
    frequency = jnp.arange(SEG // 2, dtype=jnp.int32)
    phase_index = sample_index[:, None] * frequency[None, :] % SEG
    angles = 2.0 * jnp.pi / SEG * phase_index.astype(jnp.float32)
    window = 0.5 - 0.5 * jnp.cos(2.0 * jnp.pi / SEG * sample_index.astype(jnp.float32))
    dft_basis = jnp.concatenate([jnp.cos(angles), -jnp.sin(angles)], axis=1) * window[:, None]
    return (dft_basis, jnp.sum(window * window))


def welch_spectra(pressure, welch_first):
    dft_basis, energy = welch_basis()
    half_seg = SEG // 2

    def slice_series(series, start_at):
        return jnp.stack(
            [
                lax.dynamic_slice_in_dim(series, start_at + segment_id * half_seg, SEG)
                for segment_id in range(NSEG)
            ]
        )

    segments = jax.vmap(slice_series)(pressure, welch_first)
    num_rows = pressure.shape[0]
    coeffs = jnp.dot(
        segments.reshape(num_rows * NSEG, SEG),
        dft_basis,
        precision=lax.Precision.HIGHEST,
        preferred_element_type=jnp.float32,
    )
    power = coeffs[:, :half_seg] ** 2 + coeffs[:, half_seg:] ** 2
    return jnp.mean(power.reshape(num_rows, NSEG, half_seg), axis=1) / energy


def general_device(surface_nodes, amplitudes, block_offsets, welch_first):
    cycle_size = lax.axis_size("az")
    position = lax.axis_index("az")
    observers = NO // cycle_size
    own_rows = surface_nodes.reshape(4 * NAXIAL, surface_nodes.shape[-1])
    own_table = amplitudes.reshape(KTAPS, NO, 4 * NAXIAL)
    own_offsets = block_offsets[0]
    following = shifted(surface_nodes, "az", -1)
    next_rows = following.reshape(4 * NAXIAL, following.shape[-1])
    sources = [(own_table, own_offsets, [own_rows, next_rows])]

    def observer_term(obs_block, length):
        amp_table, offset_row, node_list = sources[0]
        chosen = lax.dynamic_slice_in_dim(amp_table, obs_block * observers, observers, axis=1)
        summed = pair_term(
            node_list, chosen.reshape(KTAPS * observers, 4 * NAXIAL), offset_row[obs_block], length
        )
        return summed

    def advance(step_id, carried):
        obs_block = (position - 1 - step_id) % cycle_size
        return shifted(carried + observer_term(obs_block, NSAMP), "az", 1)

    carried = lax.fori_loop(0, cycle_size - 1, advance, jnp.zeros((observers, NSAMP), jnp.float32))
    pressure = carried + observer_term(position, NSAMP)
    spectra = welch_spectra(pressure, welch_first)
    return (pressure, spectra)


NSRC = NSAMP + HEAD
CHUNK = 256
N_IN = NSRC // CHUNK
N_OUT = NSAMP // CHUNK
NZ = 4
OBS = 16
MESH = pl.DeviceIdType.MESH


def basis_parts():
    n = np.arange(SEG)
    f = np.arange(SEG // 2)
    angles = 2.0 * np.pi / SEG * ((n[:, None] * f[None, :]) % SEG)
    window = 0.5 - 0.5 * np.cos(2.0 * np.pi / SEG * n)
    basis = np.concatenate([np.cos(angles), -np.sin(angles)], axis=1) * window[:, None]
    high = basis.astype(np.float32).astype(ml_dtypes.bfloat16)
    low = (basis - high.astype(np.float64)).astype(np.float32).astype(ml_dtypes.bfloat16)
    return np.stack([high, low]), float(np.sum(window * window))


def moved(part, distance, levels, width):
    for level in range(levels - 1, 6, -1):
        step = 1 << level
        size = part.shape[1] - (step if step < 1 << (levels - 1) else 0)
        chosen = (distance[:, :size] & step) != 0
        if size == part.shape[1]:
            ahead = jnp.concatenate([part[:, step:], part[:, :step]], axis=1)
        else:
            ahead = part[:, step:]
        part = jnp.where(chosen, ahead, part[:, :size])
    size = part.shape[1]
    for level in range(7):
        step = 1 << level
        part = jnp.where((distance[:, :size] & step) != 0, pltpu.roll(part, size - step, axis=1), part)
    return part[:, :width]


def fused(
    energy,
    offs, first, nodes, amps, basis_hbm,
    pressure_out, spectra_out,
    own, following, basis, carry, series, terms, got_core, got_y, got_z, padded,
    x_send, x_recv, c_send, c_recv, y_send, y_recv, z_send, z_recv, local_sem,
):
    me = lax.axis_index("az")
    core = lax.rem(me, 2)
    y = lax.rem(me // 2, 2)
    z = me // 4
    left = lax.rem(me + 15, 16)
    right = lax.rem(me + 1, 16)
    sibling = z * 4 + y * 2 + (1 - core)
    across = z * 4 + (1 - y) * 2 + core

    def along(r):
        return lax.rem(z + r, NZ) * 4 + y * 2 + core

    own_copy = pltpu.make_async_copy(nodes, own, local_sem.at[0])
    own_copy.start()
    basis_copy = pltpu.make_async_copy(basis_hbm, basis, local_sem.at[1])
    basis_copy.start()

    barrier = pltpu.get_barrier_semaphore()
    for partner in (left, right, across, along(1), along(2), along(3)):
        pl.semaphore_signal(barrier, inc=1, device_id={"az": partner}, device_id_type=MESH)
    pl.semaphore_wait(barrier, 6)

    def remote(src, dst, send, recv, target):
        return pltpu.make_async_remote_copy(
            src_ref=src, dst_ref=dst, send_sem=send, recv_sem=recv,
            device_id={"az": target}, device_id_type=MESH,
        )

    x_copies = []
    for j in range(N_IN):
        cols = pl.ds(j * CHUNK, CHUNK)
        x_copies.append(remote(nodes.at[:, :, cols], following.at[:, :, cols], x_send.at[j], x_recv.at[j], left))
        x_copies[-1].start()

    carry[...] = jnp.zeros_like(carry)
    lane0 = lax.broadcasted_iota(jnp.int32, (32, 128), 1) == 0
    own_copy.wait()

    def delayed(j):
        cols = pl.ds(j * CHUNK, CHUNK)

        def body(pair, _):
            rows = pl.ds(pl.multiple_of(pair * 32, 32), 32)
            a = amps[:, rows, :].reshape(KTAPS * 32, 4 * NAXIAL)
            d = jnp.dot(a, own[:, :, cols].reshape(4 * NAXIAL, CHUNK), preferred_element_type=jnp.float32)
            d = d + jnp.dot(a, following[:, :, cols].reshape(4 * NAXIAL, CHUNK), preferred_element_type=jnp.float32)
            d = d.reshape(KTAPS, 32, CHUNK)
            total = d[KTAPS - 1]
            for m in range(KTAPS - 2, -1, -1):
                turned = pltpu.roll(total, 1, axis=1)
                before = carry[m, rows, :]
                carry[m, rows, :] = turned[:, :128]
                lead = jnp.where(lane0, before, turned[:, :128])
                total = d[m] + jnp.concatenate([lead, turned[:, 128:]], axis=1)
            series[rows, cols] = 0.5 * total
            return 0

        lax.fori_loop(0, NO // 32, body, 0)

    def make_terms(q):
        def body(b, _):
            offset = offs[0, b]
            shift = HEAD - jnp.maximum(offset, 0)
            rows = pl.ds(pl.multiple_of(b * OBS, OBS), OBS)
            part = series[rows, pl.ds(q * CHUNK, CHUNK + HEAD)]
            part = moved(part, jnp.full((OBS, CHUNK + HEAD), shift, jnp.int32), 9, CHUNK)
            part = jnp.where(jnp.full((OBS, CHUNK), offset, jnp.int32) >= 0, part, 0.0)
            terms[q, lax.rem(b, 2), lax.rem(b // 2, 2), b // 4] = part
            return 0

        lax.fori_loop(0, 16, body, 0)

    c_copies, y_copies, z_copies = [], [], []
    for j in range(N_IN + 4):
        if j < N_IN:
            x_copies[j].wait_recv()
            delayed(j)
        q = j - 1
        if 0 <= q < N_OUT:
            make_terms(q)
            c_copies.append(remote(terms.at[q, 1 - core], got_core.at[q], c_send.at[q], c_recv.at[q], sibling))
            c_copies[q].start()
        q = j - 2
        if 0 <= q < N_OUT:
            c_copies[q].wait_recv()
            terms[q, core] = terms[q, core] + got_core[q]
            y_copies.append(remote(terms.at[q, core, 1 - y], got_y.at[q], y_send.at[q], y_recv.at[q], across))
            y_copies[q].start()
        q = j - 3
        if 0 <= q < N_OUT:
            y_copies[q].wait_recv()
            terms[q, core, y] = terms[q, core, y] + got_y[q]
            z_copies.append([])
            for r in range(1, NZ):
                z_copies[q].append(
                    remote(terms.at[q, core, y, lax.rem(z + r, NZ)], got_z.at[q, r - 1], z_send.at[q, r - 1], z_recv.at[q, r - 1], along(r))
                )
                z_copies[q][-1].start()
        q = j - 4
        if 0 <= q < N_OUT:
            result = terms[q, core, y, z]
            for r in range(1, NZ):
                z_copies[q][r - 1].wait_recv()
                result = result + got_z[q, r - 1]
            cols = pl.ds(q * CHUNK, CHUNK)
            padded[:, cols] = result
            pressure_out[:, cols] = result

    width = SEG + SEG // 2

    row_ids = lax.broadcasted_iota(jnp.int32, (OBS, NSAMP), 0)
    distance = jnp.zeros((OBS, NSAMP), jnp.int32)
    for o in range(OBS):
        distance = jnp.where(row_ids == o, first[o], distance)
    segments = moved(padded[...], distance, 10, width)
    basis_copy.wait()
    both = jnp.concatenate([segments[:, :SEG], segments[:, SEG // 2 : width]], axis=0)
    high = both.astype(jnp.bfloat16)
    low = (both - high.astype(jnp.float32)).astype(jnp.bfloat16)
    stacked = jnp.concatenate([high, low], axis=0)
    for f in range(0, SEG // 2, CHUNK):
        power = None
        for base in (0, SEG // 2):
            cols = pl.ds(base + f, CHUNK)
            main = jnp.dot(stacked, basis[0, :, cols], preferred_element_type=jnp.float32)
            rest = jnp.dot(high, basis[1, :, cols], preferred_element_type=jnp.float32)
            coeffs = main[: 2 * OBS] + main[2 * OBS :] + rest
            power = coeffs * coeffs if power is None else power + coeffs * coeffs
        spectra_out[:, pl.ds(f, CHUNK)] = (power[:OBS] + power[OBS:]) * (0.5 / energy)

    for copy in x_copies + c_copies + y_copies + sum(z_copies, []):
        copy.wait_send()


def fast_device(surface_nodes, amplitudes, block_offsets, welch_first):
    basis, energy = basis_parts()
    nodes = surface_nodes.reshape(4, NAXIAL, NSRC)
    amps = amplitudes.reshape(KTAPS, NO, 4 * NAXIAL)
    vmem = pl.BlockSpec(memory_space=pltpu.VMEM)
    smem = pl.BlockSpec(memory_space=pltpu.SMEM)
    anywhere = pl.BlockSpec(memory_space=pl.ANY)
    dma = pltpu.SemaphoreType.DMA
    f32 = jnp.float32
    return pl.pallas_call(
        functools.partial(fused, energy),
        out_shape=(
            jax.ShapeDtypeStruct((OBS, NSAMP), f32),
            jax.ShapeDtypeStruct((OBS, SEG // 2), f32),
        ),
        in_specs=[smem, smem, anywhere, vmem, anywhere],
        out_specs=(vmem, vmem),
        scratch_shapes=[
            pltpu.VMEM((4, NAXIAL, NSRC), jnp.bfloat16),
            pltpu.VMEM((4, NAXIAL, NSRC), jnp.bfloat16),
            pltpu.VMEM((2, SEG, SEG), jnp.bfloat16),
            pltpu.VMEM((KTAPS - 1, NO, 128), f32),
            pltpu.VMEM((NO, NSRC), f32),
            pltpu.VMEM((N_OUT, 2, 2, NZ, OBS, CHUNK), f32),
            pltpu.VMEM((N_OUT, 2, NZ, OBS, CHUNK), f32),
            pltpu.VMEM((N_OUT, NZ, OBS, CHUNK), f32),
            pltpu.VMEM((N_OUT, NZ - 1, OBS, CHUNK), f32),
            pltpu.VMEM((OBS, NSAMP), f32),
            dma((N_IN,)), dma((N_IN,)),
            dma((N_OUT,)), dma((N_OUT,)),
            dma((N_OUT,)), dma((N_OUT,)),
            dma((N_OUT, NZ - 1)), dma((N_OUT, NZ - 1)),
            dma((2,)),
        ],
        compiler_params=pltpu.CompilerParams(
            collective_id=0, has_side_effects=True, vmem_limit_bytes=44 * 1024 * 1024
        ),
    )(block_offsets, welch_first, nodes, amps, jnp.asarray(basis))


def solution(mesh):
    placed = (
        P("groups", "az", None, None),
        P("groups", None, None, "az", None),
        P("az", "groups"),
        P(("groups", "az")),
    )
    return jax.shard_map(
        fast_device if mesh.shape["az"] == 16 else general_device,
        mesh=mesh,
        in_specs=placed,
        out_specs=(P(("groups", "az"), None), P(("groups", "az"), None)),
        check_vma=False,
    )
```

```python
import functools

import jax
import jax.numpy as jnp
import ml_dtypes
import numpy as np
from jax import lax
from jax.experimental import pallas as pl
from jax.experimental.pallas import tpu as pltpu
from jax.sharding import PartitionSpec as P

NAXIAL = 128
NO = 256
KTAPS = 8
HEAD = 256
SEG = 1024
NSEG = 2
NSAMP = 2048


def shifted(block, axis, distance):
    devices = range(lax.axis_size(axis))
    route = [((i - distance) % len(devices), i) for i in devices]
    return lax.ppermute(block, axis, route)


def pair_term(node_list, amp_rows, offset, length):
    observers = amp_rows.shape[0] // KTAPS

    def compute():
        delayed = jnp.zeros((amp_rows.shape[0], length + HEAD), jnp.float32)
        for node_rows in node_list:
            delayed = delayed + jnp.dot(amp_rows, node_rows, preferred_element_type=jnp.float32)
        delayed = (0.5 * delayed).reshape(KTAPS, observers, length + HEAD)
        summed = jnp.zeros((observers, length), jnp.float32)
        for tap_index in range(KTAPS):
            summed = summed + lax.dynamic_slice_in_dim(
                delayed[tap_index], HEAD - offset - tap_index, length, axis=1
            )
        return summed

    def skipped():
        return jnp.zeros((observers, length), jnp.float32)

    return lax.cond(offset >= 0, compute, skipped)


def welch_basis():
    sample_index = jnp.arange(SEG, dtype=jnp.int32)
    frequency = jnp.arange(SEG // 2, dtype=jnp.int32)
    phase_index = sample_index[:, None] * frequency[None, :] % SEG
    angles = 2.0 * jnp.pi / SEG * phase_index.astype(jnp.float32)
    window = 0.5 - 0.5 * jnp.cos(2.0 * jnp.pi / SEG * sample_index.astype(jnp.float32))
    dft_basis = jnp.concatenate([jnp.cos(angles), -jnp.sin(angles)], axis=1) * window[:, None]
    return (dft_basis, jnp.sum(window * window))


def welch_spectra(pressure, welch_first):
    dft_basis, energy = welch_basis()
    half_seg = SEG // 2

    def slice_series(series, start_at):
        return jnp.stack(
            [
                lax.dynamic_slice_in_dim(series, start_at + segment_id * half_seg, SEG)
                for segment_id in range(NSEG)
            ]
        )

    segments = jax.vmap(slice_series)(pressure, welch_first)
    num_rows = pressure.shape[0]
    coeffs = jnp.dot(
        segments.reshape(num_rows * NSEG, SEG),
        dft_basis,
        precision=lax.Precision.HIGHEST,
        preferred_element_type=jnp.float32,
    )
    power = coeffs[:, :half_seg] ** 2 + coeffs[:, half_seg:] ** 2
    return jnp.mean(power.reshape(num_rows, NSEG, half_seg), axis=1) / energy


def general_device(surface_nodes, amplitudes, block_offsets, welch_first):
    cycle_size = lax.axis_size("az")
    position = lax.axis_index("az")
    observers = NO // cycle_size
    own_rows = surface_nodes.reshape(4 * NAXIAL, surface_nodes.shape[-1])
    own_table = amplitudes.reshape(KTAPS, NO, 4 * NAXIAL)
    own_offsets = block_offsets[0]
    following = shifted(surface_nodes, "az", -1)
    next_rows = following.reshape(4 * NAXIAL, following.shape[-1])
    sources = [(own_table, own_offsets, [own_rows, next_rows])]

    def observer_term(obs_block, length):
        amp_table, offset_row, node_list = sources[0]
        chosen = lax.dynamic_slice_in_dim(amp_table, obs_block * observers, observers, axis=1)
        summed = pair_term(
            node_list, chosen.reshape(KTAPS * observers, 4 * NAXIAL), offset_row[obs_block], length
        )
        return summed

    def advance(step_id, carried):
        obs_block = (position - 1 - step_id) % cycle_size
        return shifted(carried + observer_term(obs_block, NSAMP), "az", 1)

    carried = lax.fori_loop(0, cycle_size - 1, advance, jnp.zeros((observers, NSAMP), jnp.float32))
    pressure = carried + observer_term(position, NSAMP)
    spectra = welch_spectra(pressure, welch_first)
    return (pressure, spectra)


NSRC = NSAMP + HEAD
CHUNK = 256
N_IN = NSRC // CHUNK
N_OUT = NSAMP // CHUNK
NZ = 4
OBS = 16
MESH = pl.DeviceIdType.MESH


def basis_parts():
    n = np.arange(SEG)
    f = np.arange(SEG // 2)
    angles = 2.0 * np.pi / SEG * ((n[:, None] * f[None, :]) % SEG)
    window = 0.5 - 0.5 * np.cos(2.0 * np.pi / SEG * n)
    basis = np.concatenate([np.cos(angles), -np.sin(angles)], axis=1) * window[:, None]
    high = basis.astype(np.float32).astype(ml_dtypes.bfloat16)
    low = (basis - high.astype(np.float64)).astype(np.float32).astype(ml_dtypes.bfloat16)
    return np.stack([high, low]), float(np.sum(window * window))


def moved(part, distance, levels, width):
    for level in range(levels - 1, 6, -1):
        step = 1 << level
        size = part.shape[1] - (step if step < 1 << (levels - 1) else 0)
        chosen = (distance[:, :size] & step) != 0
        if size == part.shape[1]:
            ahead = jnp.concatenate([part[:, step:], part[:, :step]], axis=1)
        else:
            ahead = part[:, step:]
        part = jnp.where(chosen, ahead, part[:, :size])
    size = part.shape[1]
    for level in range(7):
        step = 1 << level
        part = jnp.where((distance[:, :size] & step) != 0, pltpu.roll(part, size - step, axis=1), part)
    return part[:, :width]


def fused(
    energy,
    offs, first, nodes, amps, basis_hbm,
    pressure_out, spectra_out,
    own, following, basis, carry, series, terms, got_core, got_y, got_z, padded,
    x_send, x_recv, c_send, c_recv, y_send, y_recv, z_send, z_recv, local_sem,
):
    me = lax.axis_index("az")
    core = lax.rem(me, 2)
    y = lax.rem(me // 2, 2)
    z = me // 4
    left = lax.rem(me + 15, 16)
    right = lax.rem(me + 1, 16)
    sibling = z * 4 + y * 2 + (1 - core)
    across = z * 4 + (1 - y) * 2 + core

    def along(r):
        return lax.rem(z + r, NZ) * 4 + y * 2 + core

    own_copy = pltpu.make_async_copy(nodes, own, local_sem.at[0])
    own_copy.start()
    basis_copy = pltpu.make_async_copy(basis_hbm, basis, local_sem.at[1])
    basis_copy.start()

    barrier = pltpu.get_barrier_semaphore()
    for partner in (left, right, across, along(1), along(2), along(3)):
        pl.semaphore_signal(barrier, inc=1, device_id={"az": partner}, device_id_type=MESH)
    pl.semaphore_wait(barrier, 6)

    def remote(src, dst, send, recv, target):
        return pltpu.make_async_remote_copy(
            src_ref=src, dst_ref=dst, send_sem=send, recv_sem=recv,
            device_id={"az": target}, device_id_type=MESH,
        )

    x_copies = []
    for j in range(N_IN):
        cols = pl.ds(j * CHUNK, CHUNK)
        x_copies.append(remote(nodes.at[:, :, cols], following.at[:, :, cols], x_send.at[j], x_recv.at[j], left))
        x_copies[-1].start()

    carry[...] = jnp.zeros_like(carry)
    lanes = lax.broadcasted_iota(jnp.int32, (32, 128), 1)
    own_copy.wait()

    def delayed(j):
        cols = pl.ds(j * CHUNK, CHUNK)

        def body(pair, _):
            rows = pl.ds(pl.multiple_of(pair * 32, 32), 32)
            a = amps[:, rows, :].reshape(KTAPS * 32, 4 * NAXIAL)
            d = jnp.dot(a, own[:, :, cols].reshape(4 * NAXIAL, CHUNK), preferred_element_type=jnp.float32)
            d = d + jnp.dot(a, following[:, :, cols].reshape(4 * NAXIAL, CHUNK), preferred_element_type=jnp.float32)
            d = d.reshape(KTAPS, 32, CHUNK)
            total = d[0]
            for m in range(1, KTAPS):
                turned = pltpu.roll(d[m], m, axis=1)
                before = carry[m - 1, rows, :]
                carry[m - 1, rows, :] = turned[:, :128]
                lead = jnp.where(lanes < m, before, turned[:, :128])
                total = total + jnp.concatenate([lead, turned[:, 128:]], axis=1)
            series[rows, cols] = 0.5 * total
            return 0

        lax.fori_loop(0, NO // 32, body, 0, unroll=2)

    def make_terms(q):
        def body(level, _):
            for place in range(4):
                b = level * 4 + place
                offset = offs[0, b]
                shift = HEAD - jnp.maximum(offset, 0)
                rows = pl.ds(pl.multiple_of(b * OBS, OBS), OBS)
                part = series[rows, pl.ds(q * CHUNK, CHUNK + HEAD)]
                part = pltpu.roll(part, CHUNK + HEAD - shift, axis=1)[:, :CHUNK]
                part = jnp.where(jnp.full((OBS, CHUNK), offset, jnp.int32) >= 0, part, 0.0)
                terms[q, place % 2, place // 2, level] = part
            return 0

        lax.fori_loop(0, NZ, body, 0, unroll=2)

    c_copies, y_copies, z_copies = [], [], []
    for j in range(N_IN + 4):
        if j < N_IN:
            x_copies[j].wait_recv()
            delayed(j)
        q = j - 1
        if 0 <= q < N_OUT:
            make_terms(q)
            c_copies.append(remote(terms.at[q, 1 - core], got_core.at[q], c_send.at[q], c_recv.at[q], sibling))
            c_copies[q].start()
        q = j - 2
        if 0 <= q < N_OUT:
            c_copies[q].wait_recv()
            terms[q, core] = terms[q, core] + got_core[q]
            y_copies.append(remote(terms.at[q, core, 1 - y], got_y.at[q], y_send.at[q], y_recv.at[q], across))
            y_copies[q].start()
        q = j - 3
        if 0 <= q < N_OUT:
            y_copies[q].wait_recv()
            terms[q, core, y] = terms[q, core, y] + got_y[q]
            z_copies.append([])
            for r in range(1, NZ):
                z_copies[q].append(
                    remote(terms.at[q, core, y, lax.rem(z + r, NZ)], got_z.at[q, r - 1], z_send.at[q, r - 1], z_recv.at[q, r - 1], along(r))
                )
                z_copies[q][-1].start()
        q = j - 4
        if 0 <= q < N_OUT:
            result = terms[q, core, y, z]
            for r in range(1, NZ):
                z_copies[q][r - 1].wait_recv()
                result = result + got_z[q, r - 1]
            cols = pl.ds(q * CHUNK, CHUNK)
            padded[:, cols] = result
            pressure_out[:, cols] = result

    width = SEG + SEG // 2

    row_ids = lax.broadcasted_iota(jnp.int32, (OBS, NSAMP), 0)
    distance = jnp.zeros((OBS, NSAMP), jnp.int32)
    for o in range(OBS):
        distance = jnp.where(row_ids == o, first[o], distance)
    segments = moved(padded[...], distance, 10, width)
    basis_copy.wait()
    both = jnp.concatenate([segments[:, :SEG], segments[:, SEG // 2 : width]], axis=0)
    high = both.astype(jnp.bfloat16)
    low = (both - high.astype(jnp.float32)).astype(jnp.bfloat16)
    stacked = jnp.concatenate([high, low], axis=0)
    for f in range(0, SEG // 2, CHUNK):
        power = None
        for base in (0, SEG // 2):
            cols = pl.ds(base + f, CHUNK)
            main = jnp.dot(stacked, basis[0, :, cols], preferred_element_type=jnp.float32)
            rest = jnp.dot(high, basis[1, :, cols], preferred_element_type=jnp.float32)
            coeffs = main[: 2 * OBS] + main[2 * OBS :] + rest
            power = coeffs * coeffs if power is None else power + coeffs * coeffs
        spectra_out[:, pl.ds(f, CHUNK)] = (power[:OBS] + power[OBS:]) * (0.5 / energy)

    for copy in x_copies + c_copies + y_copies + sum(z_copies, []):
        copy.wait_send()


def fast_device(surface_nodes, amplitudes, block_offsets, welch_first):
    basis, energy = basis_parts()
    nodes = surface_nodes.reshape(4, NAXIAL, NSRC)
    amps = amplitudes.reshape(KTAPS, NO, 4 * NAXIAL)
    vmem = pl.BlockSpec(memory_space=pltpu.VMEM)
    smem = pl.BlockSpec(memory_space=pltpu.SMEM)
    anywhere = pl.BlockSpec(memory_space=pl.ANY)
    dma = pltpu.SemaphoreType.DMA
    f32 = jnp.float32
    return pl.pallas_call(
        functools.partial(fused, energy),
        out_shape=(
            jax.ShapeDtypeStruct((OBS, NSAMP), f32),
            jax.ShapeDtypeStruct((OBS, SEG // 2), f32),
        ),
        in_specs=[smem, smem, anywhere, vmem, anywhere],
        out_specs=(vmem, vmem),
        scratch_shapes=[
            pltpu.VMEM((4, NAXIAL, NSRC), jnp.bfloat16),
            pltpu.VMEM((4, NAXIAL, NSRC), jnp.bfloat16),
            pltpu.VMEM((2, SEG, SEG), jnp.bfloat16),
            pltpu.VMEM((KTAPS - 1, NO, 128), f32),
            pltpu.VMEM((NO, NSRC), f32),
            pltpu.VMEM((N_OUT, 2, 2, NZ, OBS, CHUNK), f32),
            pltpu.VMEM((N_OUT, 2, NZ, OBS, CHUNK), f32),
            pltpu.VMEM((N_OUT, NZ, OBS, CHUNK), f32),
            pltpu.VMEM((N_OUT, NZ - 1, OBS, CHUNK), f32),
            pltpu.VMEM((OBS, NSAMP), f32),
            dma((N_IN,)), dma((N_IN,)),
            dma((N_OUT,)), dma((N_OUT,)),
            dma((N_OUT,)), dma((N_OUT,)),
            dma((N_OUT, NZ - 1)), dma((N_OUT, NZ - 1)),
            dma((2,)),
        ],
        compiler_params=pltpu.CompilerParams(
            collective_id=0, has_side_effects=True, vmem_limit_bytes=44 * 1024 * 1024
        ),
    )(block_offsets, welch_first, nodes, amps, jnp.asarray(basis))


def solution(mesh):
    placed = (
        P("groups", "az", None, None),
        P("groups", None, None, "az", None),
        P("az", "groups"),
        P(("groups", "az")),
    )
    return jax.shard_map(
        fast_device if mesh.shape["az"] == 16 else general_device,
        mesh=mesh,
        in_specs=placed,
        out_specs=(P(("groups", "az"), None), P(("groups", "az"), None)),
        check_vma=False,
    )
```

```python
import functools

import jax
import jax.numpy as jnp
import ml_dtypes
import numpy as np
from jax import lax
from jax.experimental import pallas as pl
from jax.experimental.pallas import tpu as pltpu
from jax.sharding import PartitionSpec as P

NAXIAL = 128
NO = 256
KTAPS = 8
HEAD = 256
SEG = 1024
NSEG = 2
NSAMP = 2048


def shifted(block, axis, distance):
    devices = range(lax.axis_size(axis))
    route = [((i - distance) % len(devices), i) for i in devices]
    return lax.ppermute(block, axis, route)


def pair_term(node_list, amp_rows, offset, length):
    observers = amp_rows.shape[0] // KTAPS

    def compute():
        delayed = jnp.zeros((amp_rows.shape[0], length + HEAD), jnp.float32)
        for node_rows in node_list:
            delayed = delayed + jnp.dot(amp_rows, node_rows, preferred_element_type=jnp.float32)
        delayed = (0.5 * delayed).reshape(KTAPS, observers, length + HEAD)
        summed = jnp.zeros((observers, length), jnp.float32)
        for tap_index in range(KTAPS):
            summed = summed + lax.dynamic_slice_in_dim(
                delayed[tap_index], HEAD - offset - tap_index, length, axis=1
            )
        return summed

    def skipped():
        return jnp.zeros((observers, length), jnp.float32)

    return lax.cond(offset >= 0, compute, skipped)


def welch_basis():
    sample_index = jnp.arange(SEG, dtype=jnp.int32)
    frequency = jnp.arange(SEG // 2, dtype=jnp.int32)
    phase_index = sample_index[:, None] * frequency[None, :] % SEG
    angles = 2.0 * jnp.pi / SEG * phase_index.astype(jnp.float32)
    window = 0.5 - 0.5 * jnp.cos(2.0 * jnp.pi / SEG * sample_index.astype(jnp.float32))
    dft_basis = jnp.concatenate([jnp.cos(angles), -jnp.sin(angles)], axis=1) * window[:, None]
    return (dft_basis, jnp.sum(window * window))


def welch_spectra(pressure, welch_first):
    dft_basis, energy = welch_basis()
    half_seg = SEG // 2

    def slice_series(series, start_at):
        return jnp.stack(
            [
                lax.dynamic_slice_in_dim(series, start_at + segment_id * half_seg, SEG)
                for segment_id in range(NSEG)
            ]
        )

    segments = jax.vmap(slice_series)(pressure, welch_first)
    num_rows = pressure.shape[0]
    coeffs = jnp.dot(
        segments.reshape(num_rows * NSEG, SEG),
        dft_basis,
        precision=lax.Precision.HIGHEST,
        preferred_element_type=jnp.float32,
    )
    power = coeffs[:, :half_seg] ** 2 + coeffs[:, half_seg:] ** 2
    return jnp.mean(power.reshape(num_rows, NSEG, half_seg), axis=1) / energy


def general_device(surface_nodes, amplitudes, block_offsets, welch_first):
    cycle_size = lax.axis_size("az")
    position = lax.axis_index("az")
    observers = NO // cycle_size
    own_rows = surface_nodes.reshape(4 * NAXIAL, surface_nodes.shape[-1])
    own_table = amplitudes.reshape(KTAPS, NO, 4 * NAXIAL)
    own_offsets = block_offsets[0]
    following = shifted(surface_nodes, "az", -1)
    next_rows = following.reshape(4 * NAXIAL, following.shape[-1])
    sources = [(own_table, own_offsets, [own_rows, next_rows])]

    def observer_term(obs_block, length):
        amp_table, offset_row, node_list = sources[0]
        chosen = lax.dynamic_slice_in_dim(amp_table, obs_block * observers, observers, axis=1)
        summed = pair_term(
            node_list, chosen.reshape(KTAPS * observers, 4 * NAXIAL), offset_row[obs_block], length
        )
        return summed

    def advance(step_id, carried):
        obs_block = (position - 1 - step_id) % cycle_size
        return shifted(carried + observer_term(obs_block, NSAMP), "az", 1)

    carried = lax.fori_loop(0, cycle_size - 1, advance, jnp.zeros((observers, NSAMP), jnp.float32))
    pressure = carried + observer_term(position, NSAMP)
    spectra = welch_spectra(pressure, welch_first)
    return (pressure, spectra)


NSRC = NSAMP + HEAD
CHUNK = 256
N_IN = NSRC // CHUNK
N_OUT = NSAMP // CHUNK
NZ = 4
WINDOW = 2
OBS = 16
MESH = pl.DeviceIdType.MESH


def basis_parts():
    n = np.arange(SEG)
    f = np.arange(SEG // 2)
    angles = 2.0 * np.pi / SEG * ((n[:, None] * f[None, :]) % SEG)
    window = 0.5 - 0.5 * np.cos(2.0 * np.pi / SEG * n)
    basis = np.concatenate([np.cos(angles), -np.sin(angles)], axis=1) * window[:, None]
    high = basis.astype(np.float32).astype(ml_dtypes.bfloat16)
    low = (basis - high.astype(np.float64)).astype(np.float32).astype(ml_dtypes.bfloat16)
    return np.stack([high, low]), float(np.sum(window * window))


def moved(part, distance, levels, width):
    for level in range(levels - 1, 6, -1):
        step = 1 << level
        size = part.shape[1] - (step if step < 1 << (levels - 1) else 0)
        chosen = (distance[:, :size] & step) != 0
        if size == part.shape[1]:
            ahead = jnp.concatenate([part[:, step:], part[:, :step]], axis=1)
        else:
            ahead = part[:, step:]
        part = jnp.where(chosen, ahead, part[:, :size])
    size = part.shape[1]
    for level in range(7):
        step = 1 << level
        part = jnp.where((distance[:, :size] & step) != 0, pltpu.roll(part, size - step, axis=1), part)
    return part[:, :width]


def fused(
    energy,
    offs, first, nodes, amps, basis_hbm,
    pressure_out, spectra_out,
    own, following, basis, carry, series, terms, got_core, got_y, got_z, padded,
    x_send, x_recv, c_send, c_recv, y_send, y_recv, z_send, z_recv, local_sem,
):
    me = lax.axis_index("az")
    core = lax.rem(me, 2)
    y = lax.rem(me // 2, 2)
    z = me // 4
    left = lax.rem(me + 15, 16)
    right = lax.rem(me + 1, 16)
    sibling = z * 4 + y * 2 + (1 - core)
    across = z * 4 + (1 - y) * 2 + core

    def along(r):
        return lax.rem(z + r, NZ) * 4 + y * 2 + core

    own_copy = pltpu.make_async_copy(nodes, own, local_sem.at[0])
    own_copy.start()
    basis_copy = pltpu.make_async_copy(basis_hbm, basis, local_sem.at[1])
    basis_copy.start()

    barrier = pltpu.get_barrier_semaphore()
    for partner in (left, right, across, along(1), along(2), along(3)):
        pl.semaphore_signal(barrier, inc=1, device_id={"az": partner}, device_id_type=MESH)
    pl.semaphore_wait(barrier, 6)

    def remote(src, dst, send, recv, target):
        return pltpu.make_async_remote_copy(
            src_ref=src, dst_ref=dst, send_sem=send, recv_sem=recv,
            device_id={"az": target}, device_id_type=MESH,
        )

    x_copies = []
    for j in range(N_IN):
        cols = pl.ds(j * CHUNK, CHUNK)
        x_copies.append(remote(nodes.at[:, :, cols], following.at[:, :, cols], x_send.at[j], x_recv.at[j], left))
        if j < WINDOW:
            x_copies[j].start()

    carry[...] = jnp.zeros_like(carry)
    lanes = lax.broadcasted_iota(jnp.int32, (32, 128), 1)
    own_copy.wait()

    def delayed(j):
        cols = pl.ds(j * CHUNK, CHUNK)

        def body(pair, _):
            rows = pl.ds(pl.multiple_of(pair * 32, 32), 32)
            a = amps[:, rows, :].reshape(KTAPS * 32, 4 * NAXIAL)
            d = jnp.dot(a, own[:, :, cols].reshape(4 * NAXIAL, CHUNK), preferred_element_type=jnp.float32)
            d = d + jnp.dot(a, following[:, :, cols].reshape(4 * NAXIAL, CHUNK), preferred_element_type=jnp.float32)
            d = d.reshape(KTAPS, 32, CHUNK)
            total = d[0]
            for m in range(1, KTAPS):
                turned = pltpu.roll(d[m], m, axis=1)
                before = carry[m - 1, rows, :]
                carry[m - 1, rows, :] = turned[:, :128]
                lead = jnp.where(lanes < m, before, turned[:, :128])
                total = total + jnp.concatenate([lead, turned[:, 128:]], axis=1)
            series[rows, cols] = 0.5 * total
            return 0

        lax.fori_loop(0, NO // 32, body, 0, unroll=2)

    def make_terms(q):
        def body(level, _):
            for place in range(4):
                b = level * 4 + place
                offset = offs[0, b]
                shift = HEAD - jnp.maximum(offset, 0)
                rows = pl.ds(pl.multiple_of(b * OBS, OBS), OBS)
                part = series[rows, pl.ds(q * CHUNK, CHUNK + HEAD)]
                part = pltpu.roll(part, CHUNK + HEAD - shift, axis=1)[:, :CHUNK]
                part = jnp.where(jnp.full((OBS, CHUNK), offset, jnp.int32) >= 0, part, 0.0)
                terms[q, place % 2, place // 2, level] = part
            return 0

        lax.fori_loop(0, NZ, body, 0, unroll=2)

    c_copies, y_copies, z_copies = [], [], []
    for j in range(N_IN + 4):
        if j < N_IN:
            x_copies[j].wait_send()
            if j + WINDOW < N_IN:
                x_copies[j + WINDOW].start()
            x_copies[j].wait_recv()
            delayed(j)
        q = j - 1
        if 0 <= q < N_OUT:
            make_terms(q)
            c_copies.append(remote(terms.at[q, 1 - core], got_core.at[q], c_send.at[q], c_recv.at[q], sibling))
            c_copies[q].start()
        q = j - 2
        if 0 <= q < N_OUT:
            c_copies[q].wait_recv()
            terms[q, core] = terms[q, core] + got_core[q]
            y_copies.append(remote(terms.at[q, core, 1 - y], got_y.at[q], y_send.at[q], y_recv.at[q], across))
            y_copies[q].start()
        q = j - 3
        if 0 <= q < N_OUT:
            y_copies[q].wait_recv()
            terms[q, core, y] = terms[q, core, y] + got_y[q]
            z_copies.append([])
            for r in range(1, NZ):
                z_copies[q].append(
                    remote(terms.at[q, core, y, lax.rem(z + r, NZ)], got_z.at[q, r - 1], z_send.at[q, r - 1], z_recv.at[q, r - 1], along(r))
                )
                z_copies[q][-1].start()
        q = j - 4
        if 0 <= q < N_OUT:
            result = terms[q, core, y, z]
            for r in range(1, NZ):
                z_copies[q][r - 1].wait_recv()
                result = result + got_z[q, r - 1]
            cols = pl.ds(q * CHUNK, CHUNK)
            padded[:, cols] = result
            pressure_out[:, cols] = result

    width = SEG + SEG // 2

    row_ids = lax.broadcasted_iota(jnp.int32, (OBS, NSAMP), 0)
    distance = jnp.zeros((OBS, NSAMP), jnp.int32)
    for o in range(OBS):
        distance = jnp.where(row_ids == o, first[o], distance)
    segments = moved(padded[...], distance, 10, width)
    basis_copy.wait()
    both = jnp.concatenate([segments[:, :SEG], segments[:, SEG // 2 : width]], axis=0)
    high = both.astype(jnp.bfloat16)
    low = (both - high.astype(jnp.float32)).astype(jnp.bfloat16)
    stacked = jnp.concatenate([high, low], axis=0)
    for f in range(0, SEG // 2, CHUNK):
        power = None
        for base in (0, SEG // 2):
            cols = pl.ds(base + f, CHUNK)
            main = jnp.dot(stacked, basis[0, :, cols], preferred_element_type=jnp.float32)
            rest = jnp.dot(high, basis[1, :, cols], preferred_element_type=jnp.float32)
            coeffs = main[: 2 * OBS] + main[2 * OBS :] + rest
            power = coeffs * coeffs if power is None else power + coeffs * coeffs
        spectra_out[:, pl.ds(f, CHUNK)] = (power[:OBS] + power[OBS:]) * (0.5 / energy)

    for copy in c_copies + y_copies + sum(z_copies, []):
        copy.wait_send()


def fast_device(surface_nodes, amplitudes, block_offsets, welch_first):
    basis, energy = basis_parts()
    nodes = surface_nodes.reshape(4, NAXIAL, NSRC)
    amps = amplitudes.reshape(KTAPS, NO, 4 * NAXIAL)
    vmem = pl.BlockSpec(memory_space=pltpu.VMEM)
    smem = pl.BlockSpec(memory_space=pltpu.SMEM)
    anywhere = pl.BlockSpec(memory_space=pltpu.HBM)
    dma = pltpu.SemaphoreType.DMA
    f32 = jnp.float32
    return pl.pallas_call(
        functools.partial(fused, energy),
        out_shape=(
            jax.ShapeDtypeStruct((OBS, NSAMP), f32),
            jax.ShapeDtypeStruct((OBS, SEG // 2), f32),
        ),
        in_specs=[smem, smem, anywhere, vmem, anywhere],
        out_specs=(vmem, vmem),
        scratch_shapes=[
            pltpu.VMEM((4, NAXIAL, NSRC), jnp.bfloat16),
            pltpu.VMEM((4, NAXIAL, NSRC), jnp.bfloat16),
            pltpu.VMEM((2, SEG, SEG), jnp.bfloat16),
            pltpu.VMEM((KTAPS - 1, NO, 128), f32),
            pltpu.VMEM((NO, NSRC), f32),
            pltpu.VMEM((N_OUT, 2, 2, NZ, OBS, CHUNK), f32),
            pltpu.VMEM((N_OUT, 2, NZ, OBS, CHUNK), f32),
            pltpu.VMEM((N_OUT, NZ, OBS, CHUNK), f32),
            pltpu.VMEM((N_OUT, NZ - 1, OBS, CHUNK), f32),
            pltpu.VMEM((OBS, NSAMP), f32),
            dma((N_IN,)), dma((N_IN,)),
            dma((N_OUT,)), dma((N_OUT,)),
            dma((N_OUT,)), dma((N_OUT,)),
            dma((N_OUT, NZ - 1)), dma((N_OUT, NZ - 1)),
            dma((2,)),
        ],
        compiler_params=pltpu.CompilerParams(
            collective_id=0, has_side_effects=True, vmem_limit_bytes=44 * 1024 * 1024
        ),
    )(block_offsets, welch_first, nodes, amps, jnp.asarray(basis))


def solution(mesh):
    placed = (
        P("groups", "az", None, None),
        P("groups", None, None, "az", None),
        P("az", "groups"),
        P(("groups", "az")),
    )
    return jax.shard_map(
        fast_device if mesh.shape["az"] == 16 else general_device,
        mesh=mesh,
        in_specs=placed,
        out_specs=(P(("groups", "az"), None), P(("groups", "az"), None)),
        check_vma=False,
    )
```

```python
import functools

import jax
import jax.numpy as jnp
import ml_dtypes
import numpy as np
from jax import lax
from jax.experimental import pallas as pl
from jax.experimental.pallas import tpu as pltpu
from jax.sharding import PartitionSpec as P

NAXIAL = 128
NO = 256
KTAPS = 8
HEAD = 256
SEG = 1024
NSEG = 2
NSAMP = 2048


def shifted(block, axis, distance):
    devices = range(lax.axis_size(axis))
    route = [((i - distance) % len(devices), i) for i in devices]
    return lax.ppermute(block, axis, route)


def pair_term(node_list, amp_rows, offset, length):
    observers = amp_rows.shape[0] // KTAPS

    def compute():
        delayed = jnp.zeros((amp_rows.shape[0], length + HEAD), jnp.float32)
        for node_rows in node_list:
            delayed = delayed + jnp.dot(amp_rows, node_rows, preferred_element_type=jnp.float32)
        delayed = (0.5 * delayed).reshape(KTAPS, observers, length + HEAD)
        summed = jnp.zeros((observers, length), jnp.float32)
        for tap_index in range(KTAPS):
            summed = summed + lax.dynamic_slice_in_dim(
                delayed[tap_index], HEAD - offset - tap_index, length, axis=1
            )
        return summed

    def skipped():
        return jnp.zeros((observers, length), jnp.float32)

    return lax.cond(offset >= 0, compute, skipped)


def welch_basis():
    sample_index = jnp.arange(SEG, dtype=jnp.int32)
    frequency = jnp.arange(SEG // 2, dtype=jnp.int32)
    phase_index = sample_index[:, None] * frequency[None, :] % SEG
    angles = 2.0 * jnp.pi / SEG * phase_index.astype(jnp.float32)
    window = 0.5 - 0.5 * jnp.cos(2.0 * jnp.pi / SEG * sample_index.astype(jnp.float32))
    dft_basis = jnp.concatenate([jnp.cos(angles), -jnp.sin(angles)], axis=1) * window[:, None]
    return (dft_basis, jnp.sum(window * window))


def welch_spectra(pressure, welch_first):
    dft_basis, energy = welch_basis()
    half_seg = SEG // 2

    def slice_series(series, start_at):
        return jnp.stack(
            [
                lax.dynamic_slice_in_dim(series, start_at + segment_id * half_seg, SEG)
                for segment_id in range(NSEG)
            ]
        )

    segments = jax.vmap(slice_series)(pressure, welch_first)
    num_rows = pressure.shape[0]
    coeffs = jnp.dot(
        segments.reshape(num_rows * NSEG, SEG),
        dft_basis,
        precision=lax.Precision.HIGHEST,
        preferred_element_type=jnp.float32,
    )
    power = coeffs[:, :half_seg] ** 2 + coeffs[:, half_seg:] ** 2
    return jnp.mean(power.reshape(num_rows, NSEG, half_seg), axis=1) / energy


def general_device(surface_nodes, amplitudes, block_offsets, welch_first):
    cycle_size = lax.axis_size("az")
    position = lax.axis_index("az")
    observers = NO // cycle_size
    own_rows = surface_nodes.reshape(4 * NAXIAL, surface_nodes.shape[-1])
    own_table = amplitudes.reshape(KTAPS, NO, 4 * NAXIAL)
    own_offsets = block_offsets[0]
    following = shifted(surface_nodes, "az", -1)
    next_rows = following.reshape(4 * NAXIAL, following.shape[-1])
    sources = [(own_table, own_offsets, [own_rows, next_rows])]

    def observer_term(obs_block, length):
        amp_table, offset_row, node_list = sources[0]
        chosen = lax.dynamic_slice_in_dim(amp_table, obs_block * observers, observers, axis=1)
        summed = pair_term(
            node_list, chosen.reshape(KTAPS * observers, 4 * NAXIAL), offset_row[obs_block], length
        )
        return summed

    def advance(step_id, carried):
        obs_block = (position - 1 - step_id) % cycle_size
        return shifted(carried + observer_term(obs_block, NSAMP), "az", 1)

    carried = lax.fori_loop(0, cycle_size - 1, advance, jnp.zeros((observers, NSAMP), jnp.float32))
    pressure = carried + observer_term(position, NSAMP)
    spectra = welch_spectra(pressure, welch_first)
    return (pressure, spectra)


NSRC = NSAMP + HEAD
CHUNK = 256
N_IN = NSRC // CHUNK
N_OUT = NSAMP // CHUNK
NZ = 4
WINDOW = 2
OBS = 16
MESH = pl.DeviceIdType.MESH


def basis_parts():
    n = np.arange(SEG)
    f = np.arange(SEG // 2)
    angles = 2.0 * np.pi / SEG * ((n[:, None] * f[None, :]) % SEG)
    window = 0.5 - 0.5 * np.cos(2.0 * np.pi / SEG * n)
    basis = np.concatenate([np.cos(angles), -np.sin(angles)], axis=1) * window[:, None]
    high = basis.astype(np.float32).astype(ml_dtypes.bfloat16)
    low = (basis - high.astype(np.float64)).astype(np.float32).astype(ml_dtypes.bfloat16)
    return np.stack([high, low]), float(np.sum(window * window))


def moved(part, distance, levels, width):
    for level in range(levels - 1, 6, -1):
        step = 1 << level
        size = part.shape[1] - (step if step < 1 << (levels - 1) else 0)
        chosen = (distance[:, :size] & step) != 0
        if size == part.shape[1]:
            ahead = jnp.concatenate([part[:, step:], part[:, :step]], axis=1)
        else:
            ahead = part[:, step:]
        part = jnp.where(chosen, ahead, part[:, :size])
    size = part.shape[1]
    for level in range(7):
        step = 1 << level
        part = jnp.where((distance[:, :size] & step) != 0, pltpu.roll(part, size - step, axis=1), part)
    return part[:, :width]


def fused(
    energy,
    offs, first, nodes, amps, basis_hbm,
    pressure_out, spectra_out,
    own, following, basis, carry, series, terms, got_core, got_y, got_z, padded,
    x_send, x_recv, c_send, c_recv, y_send, y_recv, z_send, z_recv, local_sem,
):
    me = lax.axis_index("az")
    core = lax.rem(me, 2)
    y = lax.rem(me // 2, 2)
    z = me // 4
    left = lax.rem(me + 15, 16)
    right = lax.rem(me + 1, 16)
    sibling = z * 4 + y * 2 + (1 - core)
    across = z * 4 + (1 - y) * 2 + core

    def along(r):
        return lax.rem(z + r, NZ) * 4 + y * 2 + core

    own_copy = pltpu.make_async_copy(nodes, own, local_sem.at[0])
    own_copy.start()
    basis_copy = pltpu.make_async_copy(basis_hbm, basis, local_sem.at[1])
    basis_copy.start()

    barrier = pltpu.get_barrier_semaphore()
    for partner in (left, right, across, along(1), along(2), along(3)):
        pl.semaphore_signal(barrier, inc=1, device_id={"az": partner}, device_id_type=MESH)
    pl.semaphore_wait(barrier, 6)

    def remote(src, dst, send, recv, target):
        return pltpu.make_async_remote_copy(
            src_ref=src, dst_ref=dst, send_sem=send, recv_sem=recv,
            device_id={"az": target}, device_id_type=MESH,
        )

    x_copies = []
    for j in range(N_IN):
        cols = pl.ds(j * CHUNK, CHUNK)
        x_copies.append(remote(nodes.at[:, :, cols], following.at[:, :, cols], x_send.at[j], x_recv.at[j], left))
        if j < WINDOW:
            x_copies[j].start()

    carry[...] = jnp.zeros_like(carry)
    lanes = lax.broadcasted_iota(jnp.int32, (32, 128), 1)
    own_copy.wait()

    def delayed(j):
        cols = pl.ds(j * CHUNK, CHUNK)

        def body(pair, _):
            rows = pl.ds(pl.multiple_of(pair * 32, 32), 32)
            a = amps[:, rows, :].reshape(KTAPS * 32, 4 * NAXIAL)
            d = jnp.dot(a, own[:, :, cols].reshape(4 * NAXIAL, CHUNK), preferred_element_type=jnp.float32)
            d = d + jnp.dot(a, following[:, :, cols].reshape(4 * NAXIAL, CHUNK), preferred_element_type=jnp.float32)
            d = d.reshape(KTAPS, 32, CHUNK)
            total = d[0]
            for m in range(1, KTAPS):
                turned = pltpu.roll(d[m], m, axis=1)
                before = carry[m - 1, rows, :]
                carry[m - 1, rows, :] = turned[:, :128]
                lead = jnp.where(lanes < m, before, turned[:, :128])
                total = total + jnp.concatenate([lead, turned[:, 128:]], axis=1)
            series[rows, cols] = 0.5 * total
            return 0

        lax.fori_loop(0, NO // 32, body, 0, unroll=4)

    def make_terms(q):
        def body(level, _):
            for place in range(4):
                b = level * 4 + place
                offset = offs[0, b]
                shift = HEAD - jnp.maximum(offset, 0)
                rows = pl.ds(pl.multiple_of(b * OBS, OBS), OBS)
                part = series[rows, pl.ds(q * CHUNK, CHUNK + HEAD)]
                part = pltpu.roll(part, CHUNK + HEAD - shift, axis=1)[:, :CHUNK]
                part = jnp.where(jnp.full((OBS, CHUNK), offset, jnp.int32) >= 0, part, 0.0)
                terms[q, place % 2, place // 2, level] = part
            return 0

        lax.fori_loop(0, NZ, body, 0, unroll=4)

    c_copies, y_copies, z_copies = [], [], []
    for j in range(N_IN + 4):
        if j < N_IN:
            x_copies[j].wait_send()
            if j + WINDOW < N_IN:
                x_copies[j + WINDOW].start()
            x_copies[j].wait_recv()
            delayed(j)
        q = j - 1
        if 0 <= q < N_OUT:
            make_terms(q)
            c_copies.append(remote(terms.at[q, 1 - core], got_core.at[q], c_send.at[q], c_recv.at[q], sibling))
            c_copies[q].start()
        q = j - 2
        if 0 <= q < N_OUT:
            c_copies[q].wait_recv()
            terms[q, core] = terms[q, core] + got_core[q]
            y_copies.append(remote(terms.at[q, core, 1 - y], got_y.at[q], y_send.at[q], y_recv.at[q], across))
            y_copies[q].start()
        q = j - 3
        if 0 <= q < N_OUT:
            y_copies[q].wait_recv()
            terms[q, core, y] = terms[q, core, y] + got_y[q]
            z_copies.append([])
            for r in range(1, NZ):
                z_copies[q].append(
                    remote(terms.at[q, core, y, lax.rem(z + r, NZ)], got_z.at[q, r - 1], z_send.at[q, r - 1], z_recv.at[q, r - 1], along(r))
                )
                z_copies[q][-1].start()
        q = j - 4
        if 0 <= q < N_OUT:
            result = terms[q, core, y, z]
            for r in range(1, NZ):
                z_copies[q][r - 1].wait_recv()
                result = result + got_z[q, r - 1]
            cols = pl.ds(q * CHUNK, CHUNK)
            padded[:, cols] = result
            pressure_out[:, cols] = result

    width = SEG + SEG // 2

    row_ids = lax.broadcasted_iota(jnp.int32, (OBS, NSAMP), 0)
    distance = jnp.zeros((OBS, NSAMP), jnp.int32)
    for o in range(OBS):
        distance = jnp.where(row_ids == o, first[o], distance)
    segments = moved(padded[...], distance, 10, width)
    basis_copy.wait()
    both = jnp.concatenate([segments[:, :SEG], segments[:, SEG // 2 : width]], axis=0)
    high = both.astype(jnp.bfloat16)
    low = (both - high.astype(jnp.float32)).astype(jnp.bfloat16)
    stacked = jnp.concatenate([high, low], axis=0)
    for f in range(0, SEG // 2, CHUNK):
        power = None
        for base in (0, SEG // 2):
            cols = pl.ds(base + f, CHUNK)
            main = jnp.dot(stacked, basis[0, :, cols], preferred_element_type=jnp.float32)
            rest = jnp.dot(high, basis[1, :, cols], preferred_element_type=jnp.float32)
            coeffs = main[: 2 * OBS] + main[2 * OBS :] + rest
            power = coeffs * coeffs if power is None else power + coeffs * coeffs
        spectra_out[:, pl.ds(f, CHUNK)] = (power[:OBS] + power[OBS:]) * (0.5 / energy)

    for copy in c_copies + y_copies + sum(z_copies, []):
        copy.wait_send()


def fast_device(surface_nodes, amplitudes, block_offsets, welch_first):
    basis, energy = basis_parts()
    nodes = surface_nodes.reshape(4, NAXIAL, NSRC)
    amps = amplitudes.reshape(KTAPS, NO, 4 * NAXIAL)
    vmem = pl.BlockSpec(memory_space=pltpu.VMEM)
    smem = pl.BlockSpec(memory_space=pltpu.SMEM)
    anywhere = pl.BlockSpec(memory_space=pltpu.HBM)
    dma = pltpu.SemaphoreType.DMA
    f32 = jnp.float32
    return pl.pallas_call(
        functools.partial(fused, energy),
        out_shape=(
            jax.ShapeDtypeStruct((OBS, NSAMP), f32),
            jax.ShapeDtypeStruct((OBS, SEG // 2), f32),
        ),
        in_specs=[smem, smem, anywhere, vmem, anywhere],
        out_specs=(vmem, vmem),
        scratch_shapes=[
            pltpu.VMEM((4, NAXIAL, NSRC), jnp.bfloat16),
            pltpu.VMEM((4, NAXIAL, NSRC), jnp.bfloat16),
            pltpu.VMEM((2, SEG, SEG), jnp.bfloat16),
            pltpu.VMEM((KTAPS - 1, NO, 128), f32),
            pltpu.VMEM((NO, NSRC), f32),
            pltpu.VMEM((N_OUT, 2, 2, NZ, OBS, CHUNK), f32),
            pltpu.VMEM((N_OUT, 2, NZ, OBS, CHUNK), f32),
            pltpu.VMEM((N_OUT, NZ, OBS, CHUNK), f32),
            pltpu.VMEM((N_OUT, NZ - 1, OBS, CHUNK), f32),
            pltpu.VMEM((OBS, NSAMP), f32),
            dma((N_IN,)), dma((N_IN,)),
            dma((N_OUT,)), dma((N_OUT,)),
            dma((N_OUT,)), dma((N_OUT,)),
            dma((N_OUT, NZ - 1)), dma((N_OUT, NZ - 1)),
            dma((2,)),
        ],
        compiler_params=pltpu.CompilerParams(
            collective_id=0, has_side_effects=True, vmem_limit_bytes=44 * 1024 * 1024
        ),
    )(block_offsets, welch_first, nodes, amps, jnp.asarray(basis))


def solution(mesh):
    placed = (
        P("groups", "az", None, None),
        P("groups", None, None, "az", None),
        P("az", "groups"),
        P(("groups", "az")),
    )
    return jax.shard_map(
        fast_device if mesh.shape["az"] == 16 else general_device,
        mesh=mesh,
        in_specs=placed,
        out_specs=(P(("groups", "az"), None), P(("groups", "az"), None)),
        check_vma=False,
    )
```
